32 devices in a mesh: row: 8 (over y, x, core), col: 4 (over z).
Axes of the slice: x: 2, y: 2, z: 4, core: 2. Of those that a mesh axis runs over, the one named last changes fastest.
Arguments:
- k_vals: float32 [128, 15, 64, 64], P('row'), may hold values from -0.1875 to 0.1875
- k_cols: int32 [128, 15], P('row'), may hold values from -8 to 135, as said below
- p_vals: float32 [128, 3, 64, 64], P('row', None, None, 'col'), may hold values from -1.2 to 1.2
- p_cols: int32 [128, 3], P('row'), may hold values from -1 to 15, as said below
Outputs:
- coarse: float32 [16, 7, 64, 64], P('row', None, None, 'col')
The draws below stay inside these ranges and needn't reach their ends.
Inputs may be any that keep to these rules, and one draw needn't show every extreme that they name: Each k_cols[i, s] - i lies between -8 and 8; within a block row the columns differ; a column outside 0 to 127 stands for an absent block. Each p_cols[k, s] is -1 for an absent block or lies within 1 of k // 8, the aggregate of block row k; the present columns of a row differ, and the aggregate of every block row is present.
All inputs are finite; a program needn't handle non-finite values.
Results may differ from the reference program's by a relative error of at most 0.0001.
Values sent between devices are 32-bit elements; how exact they have to be, the bound alone decides.
No kernel may reach another device: no remote copies, remote signals or barrier semaphores. Data moves between devices by JAX's collectives and lax.ppermute only.
A program may use at most 128 MiB of HBM per device.

```python
import jax
import jax.numpy as jnp
from jax import lax

B = 64
CB = 64
KNZ = 15
AGG = 8
PNZ = 3
NB = 128


def draw_k_cols(key, part):
    reach = AGG
    span = 2 * reach - 2
    scores = jax.random.randint(key, (NB, span), 0, 1 << 20) * span + jnp.arange(span)[None, :]
    order = jnp.argsort(scores, axis=1)
    chosen = order[:, :KNZ - 3]
    candidates = jnp.concatenate([jnp.arange(-(reach - 1), 0), jnp.arange(1, reach)])
    offsets = candidates[chosen]
    fixed = jnp.broadcast_to(jnp.array([0, -reach, reach]), (NB, 3))
    block_rows = jnp.arange(NB)[:, None]
    return (block_rows + jnp.concatenate([fixed, offsets], axis=1)).astype(jnp.int32)


def draw_p_cols(key, part):
    first_key = jax.random.fold_in(key, 11)
    second_key = jax.random.fold_in(key, 23)
    scores = jax.random.randint(first_key, (NB, 3), 0, 1 << 20) * 3 + jnp.arange(3)[None, :]
    offsets = jnp.argsort(scores, axis=1) - 1
    keeper = jax.random.randint(second_key, (NB, 3), 0, 3) > 0
    keeper = keeper | (offsets == 0)
    aggregate = jnp.arange(NB)[:, None] // AGG
    columns = aggregate + offsets
    inside = (columns >= 0) & (columns < NB // AGG)
    return jnp.where(keeper & inside, columns, -1).astype(jnp.int32)


def shard_levels(own_key, shape, cuts, least, largest):
    def one(dim, blocks):
        draws = jax.random.uniform(jax.random.fold_in(jax.random.fold_in(own_key, 6), dim), (blocks,), jnp.float32, least / len(cuts), largest / len(cuts))
        return jnp.repeat(jnp.exp(draws), shape[dim] // blocks).reshape((-1,) + (1,) * (len(shape) - dim - 1))

    gain = one(*cuts[0])
    for cut in cuts[1:]:
        gain = gain * one(*cut)
    return gain


def bell_draw(rng, shape, scale, most, split=(), kind=jnp.bfloat16):
    values = jax.random.normal(rng, shape, jnp.float32) * scale
    if len(split) > 0:
        values = shard_levels(rng, shape, split, -0.22, 0.18) * values
    return jnp.clip(values, min=-most, max=most).astype(kind)


def setup_inputs(seed: int = 0) -> dict:
    key_of = jax.random.split(jax.random.key(seed), 5)
    return {
        "k_vals": bell_draw(key_of[0], (NB, KNZ, B, B), (B * KNZ) ** -0.5, 0.1875, ((0, 8),), jnp.float32),
        "k_cols": draw_k_cols(jax.random.fold_in(key_of[4], 71), 0),
        "p_vals": bell_draw(key_of[2], (NB, PNZ, B, CB), 0.2, 1.2, ((0, 8), (3, 4)), jnp.float32),
        "p_cols": draw_p_cols(jax.random.fold_in(key_of[4], 71), 0),
    }


def place_window(p_vals, p_cols, aggregate, blocks_all):
    present = (p_cols >= 0) & (p_cols < blocks_all)
    position = p_cols - aggregate[:, None] + 1
    selector = ((position[:, :, None] == jnp.arange(3, dtype=jnp.int32)[None, None, :]) & present[:, :, None]).astype(jnp.float32)
    return jnp.einsum("jtu,jtbc->jubc", selector, p_vals, precision=lax.Precision.HIGHEST)


def reference(k_vals, k_cols, p_vals, p_cols):
    total_rows = k_vals.shape[0]
    blocks_all = total_rows // AGG
    width = p_vals.shape[3]
    aggregate = jnp.arange(total_rows, dtype=jnp.int32) // AGG
    window = place_window(p_vals, p_cols, aggregate, blocks_all)
    in_range = (k_cols >= 0) & (k_cols < total_rows)
    safe_cols = jnp.clip(k_cols, 0, total_rows - 1).astype(jnp.int32)
    near_agg = safe_cols // AGG - aggregate[:, None] + 1
    side_mask = ((near_agg[:, :, None] == jnp.arange(3, dtype=jnp.int32)[None, None, :]) & in_range[:, :, None]).astype(jnp.float32)

    def one_row(triple):
        blocks, columns, masks = triple
        pieces = jnp.take(window, columns, axis=0)
        product = jnp.einsum("sab,subc->suac", blocks, pieces, precision=lax.Precision.HIGHEST)
        mixed_terms = jnp.einsum("se,suac->euac", masks, product, precision=lax.Precision.HIGHEST)
        result = jnp.zeros((5,) + mixed_terms.shape[2:], jnp.float32)
        for offset in range(3):
            result = result.at[offset:offset + 3].add(mixed_terms[offset])
        return result

    stiff_prolong = lax.map(one_row, (k_vals, safe_cols, side_mask))
    coarse = jnp.zeros((blocks_all, 7, width, width), jnp.float32)
    empty_row = jnp.zeros((1, width, width), jnp.float32)
    for left_slot in range(3):
        for right_slot in range(5):
            term = jnp.einsum("ibc,ibd->icd", window[:, left_slot], stiff_prolong[:, right_slot], precision=lax.Precision.HIGHEST)
            term = term.reshape(blocks_all, AGG, width, width).sum(axis=1)
            if left_slot == 0:
                moved = jnp.concatenate([term[1:], empty_row], axis=0)
            elif left_slot == 1:
                moved = term
            else:
                moved = jnp.concatenate([empty_row, term[:-1]], axis=0)
            coarse = coarse.at[:, right_slot - left_slot + 2].add(moved)
    return coarse
```

```python
import functools

import jax
import jax.numpy as jnp
from jax import lax
from jax.experimental import pallas as pl
from jax.experimental.pallas import tpu as pltpu
from jax.sharding import PartitionSpec as P

AGG = 8
PAIRS = AGG // 2


def split_high_low(value):
    high = value.astype(jnp.bfloat16)
    low = (value - high.astype(jnp.float32)).astype(jnp.bfloat16)
    return high, low


def pack_kernel(
    blocks_all, cols_hbm, p_hbm, both_ref, mine_ref, other_ref, mine_again, other_again,
    cols_ref, p_ref, sems,
):
    cols_copy = pltpu.make_async_copy(cols_hbm, cols_ref, sems.at[0])
    p_copy = pltpu.make_async_copy(p_hbm, p_ref, sems.at[1])
    cols_copy.start()
    p_copy.start()
    half = lax.axis_index("col") % 2
    first_agg = lax.axis_index("row") * 2
    blank = jnp.zeros(p_ref.shape[2:], jnp.float32)
    cols_copy.wait()
    p_copy.wait()
    for part, out_ref, again in ((0, mine_ref, mine_again), (1, other_ref, other_again)):
        group = half if part == 0 else 1 - half
        targets = []
        for window in range(3):
            target = first_agg + group - 1 + window
            targets.append(jnp.where((target >= 0) & (target < blocks_all), target, -2))
        for pair in range(PAIRS):
            rows = []
            for sub in range(2):
                row = group * AGG + 2 * pair + sub
                rows.append([(cols_ref[slot, row], p_ref[row, slot]) for slot in range(3)])
            for window, target in enumerate(targets):
                halves = []
                for slots in rows:
                    value = blank
                    for column, block in slots:
                        value = jnp.where(column == target, block, value)
                    halves.append(value)
                packed = jnp.concatenate(halves, axis=1)
                out_ref[pair, window] = packed
                again[pair, window] = packed
                both_ref[part * PAIRS + pair, window] = packed


def split_kernel(slots, total_rows, cols_hbm, k_hbm, out_ref, cols_ref, k_ref, cols_sem, sems):
    half = lax.axis_index("col") % 2
    first_row = lax.axis_index("row") * (2 * AGG) + half * AGG
    absent = 3 * AGG

    def k_copy(row):
        return pltpu.make_async_copy(k_hbm.at[half * AGG + row], k_ref.at[row], sems.at[row])

    cols_copy = pltpu.make_async_copy(cols_hbm, cols_ref, cols_sem)
    cols_copy.start()
    for row in range(AGG):
        k_copy(row).start()

    def one_blank(row, carry):
        for column in range(absent):
            out_ref[row, column] = jnp.zeros((64, 128), jnp.bfloat16)
        return carry

    lax.fori_loop(0, AGG, one_blank, 0)
    cols_copy.wait()

    def one_row(row, carry):
        k_copy(row).wait()
        for slot in range(slots):
            column = cols_ref[half * AGG + row, slot]
            present = (column >= 0) & (column < total_rows)
            place = jnp.where(present, column - first_row + AGG, absent)
            place = jnp.clip(place, 0, absent)
            out_ref[row, place] = jnp.concatenate(split_high_low(k_ref[row, slot]), axis=1)
        return carry

    lax.fori_loop(0, AGG, one_row, 0)


def transpose_blocks(sources, place_ref, p_ref):
    depth = place_ref.shape[1] * place_ref.shape[2] * place_ref.shape[3]
    for side, (source, first) in enumerate(sources):
        for pair in range(PAIRS):
            for window in range(3):
                place_ref[pair, window, side] = source[first + pair, window]
    for pair in range(PAIRS):
        turned = place_ref[pair].reshape(depth, 128).T
        for place, part in enumerate(split_high_low(turned)):
            for sub in range(2):
                p_ref[2 * pair + sub, :, 128 * place : 128 * place + depth] = part[
                    64 * sub : 64 * sub + 64
                ]


def stiff_product(step, k_ref, p_ref):
    rows = []
    blocks = []
    for row in range(AGG):
        rows.append(k_ref[:, step * AGG + row].reshape(AGG * 64, 128))
        blocks += [p_ref[row], p_ref[row]]
    total = jnp.dot(
        jnp.concatenate(rows, axis=1),
        jnp.concatenate(blocks, axis=0),
        preferred_element_type=jnp.float32,
    )
    return split_high_low(total[:, :128] + total[:, 128:])


def stiff_kernel(mine, other, pair_both, k_ref, out_ref, place_ref, p_ref):
    half = lax.axis_index("col") % 2
    for place, step, sources in (
        (0, 1, ((mine, 0), (pair_both, PAIRS))),
        (1, 2 - 2 * half, ((other, 0), (pair_both, 0))),
    ):
        transpose_blocks(sources, place_ref.at[place], p_ref.at[place])
        high, low = stiff_product(step, k_ref, p_ref.at[place])
        out_ref[place, 0] = high
        out_ref[place, 1] = low


def coarse_terms(stiffs, pieces, windows, share, high_ref, low_ref):
    count = len(pieces)
    width = count * share
    depth = 6 * share
    position = lax.axis_index("col")
    first_half = position % 2 == 0
    for place, window in enumerate(windows):
        for shift in range(count):
            first = PAIRS if shift == 1 else 0
            for pair in range(PAIRS):
                high, low = split_high_low(pieces[shift][first + pair, window])
                high_ref[place, pair, position ^ shift] = high
                low_ref[place, pair, position ^ shift] = low

    def rows_of(part):
        return jnp.concatenate(
            [
                jnp.concatenate(
                    [part[place, pair].reshape(width, 128) for pair in range(PAIRS)], axis=1
                )
                for place in range(len(windows))
            ],
            axis=0,
        )

    high, low = rows_of(high_ref), rows_of(low_ref)
    both = jnp.concatenate([high, low], axis=0)
    rows = len(windows) * width
    totals = []
    for stiff_high, stiff_low in stiffs:
        total = jnp.dot(both, stiff_high, preferred_element_type=jnp.float32)
        rest = jnp.dot(high, stiff_low, preferred_element_type=jnp.float32)
        totals.append(total[:rows] + total[rows:] + rest)
    mine, other, near = totals
    steps = (jnp.where(first_half, near, other), mine, jnp.where(first_half, other, near))
    terms = [[None] * 5 for _ in windows]
    for step, total in enumerate(steps):
        for place in range(len(windows)):
            turned = total[width * place : width * place + width].T[:depth]
            turned = turned.reshape(3, 2, share, width)
            for slot in range(3):
                before = terms[place][step + slot]
                terms[place][step + slot] = turned[slot] if before is None else before + turned[slot]
    return terms


def edge_kernel(count, share, k_ref, stiff, *refs):
    pieces = refs[:count]
    near, pair_near, edge_ref, near_ref, place_ref, p_ref, high_ref, low_ref = refs[count:]
    half = lax.axis_index("col") % 2
    transpose_blocks(((near, 0), (pair_near, 0)), place_ref, p_ref)
    high, low = stiff_product(2 * half, k_ref, p_ref)
    near_ref[0] = high
    near_ref[1] = low
    stiffs = [(stiff[place, 0], stiff[place, 1]) for place in range(2)] + [(high, low)]
    (terms,) = coarse_terms(stiffs, pieces, (2 * half,), share, high_ref, low_ref)
    for slot in range(5):
        for side in range(2):
            term = terms[slot][side]
            folded = jnp.concatenate([term[: share // 2], term[share // 2 :]], axis=1)
            edge_ref[5 * side + slot] = folded


def inner_kernel(count, share, stiff, stiff_near, *refs):
    pieces = refs[:count]
    own_ref, pair_ref, high_ref, low_ref = refs[count:]
    half = lax.axis_index("col") % 2
    width = count * share
    stiffs = [(stiff[place, 0], stiff[place, 1]) for place in range(2)]
    stiffs.append((stiff_near[0], stiff_near[1]))
    windows = (1 - half, 2 - half)
    lower, upper = coarse_terms(stiffs, pieces, windows, share, high_ref, low_ref)
    for side, ref in ((0, own_ref), (1, pair_ref)):
        for slot in range(5):
            ref[slot] = jnp.concatenate([lower[slot][side], upper[slot][side]], axis=1)


def sum_kernel(share, own, from_pair, from_edge, from_pair_edge, out_ref):
    half = lax.axis_index("col") % 2
    width = own.shape[2] // 2

    def unfold(folded):
        return jnp.concatenate([folded[:, :width], folded[:, width:]], axis=0)

    def write(lower, upper, before, after):
        for offset in range(7):
            first = [lower[offset - 1][:, :width]] if 1 <= offset < 6 else []
            first += [upper[offset - 2][:, :width]] if 2 <= offset else []
            first += [unfold(before[offset])] if offset < 5 else []
            out_ref[0, offset] = sum(first[1:], first[0])
            second = [lower[offset][:, width:]] if offset < 5 else []
            second += [upper[offset - 1][:, width:]] if 1 <= offset < 6 else []
            second += [unfold(after[offset - 2])] if 2 <= offset else []
            out_ref[1, offset] = sum(second[1:], second[0])

    @pl.when(half == 0)
    def _():
        write(own, from_pair, from_pair_edge, from_edge)

    @pl.when(half == 1)
    def _():
        write(from_pair, own, from_edge, from_pair_edge)


def body(k_vals, k_cols, p_vals, p_cols, *, rows_axis, cols_axis):
    own_rows, slots, fine, _ = k_vals.shape
    share = p_vals.shape[3]
    padded = -(-share // 16) * 16
    total_rows = own_rows * rows_axis
    blocks_all = total_rows // AGG
    width = cols_axis * padded
    vmem = pl.BlockSpec(memory_space=pltpu.VMEM)
    hbm = pl.BlockSpec(memory_space=pltpu.HBM)
    params = pltpu.CompilerParams(vmem_limit_bytes=24 * 1024 * 1024)

    def in_hbm(value):
        return pltpu.with_memory_space_constraint(value, pltpu.HBM)

    def send(value, target):
        perm = []
        for row in range(rows_axis):
            for col in range(cols_axis):
                to_row, to_col = target(row, col)
                perm.append((row * cols_axis + col, to_row * cols_axis + to_col))
        return lax.ppermute(value, ("row", "col"), perm)

    def toward(row, col):
        return (row + (1 if col % 2 == 0 else -1)) % rows_axis, col

    def away(row, col):
        to_row = row - (1 if col % 2 == 0 else -1)
        return (to_row, col) if 0 <= to_row < rows_axis else swap(row, col)

    def swap(row, col):
        return row, col ^ 1

    p_rows = jnp.swapaxes(p_vals, 2, 3)
    if padded != share:
        p_rows = jnp.pad(p_rows, ((0, 0), (0, 0), (0, padded - share), (0, 0)))
    group_shape = jax.ShapeDtypeStruct((PAIRS, 3, padded, 128), jnp.float32)
    both_shape = jax.ShapeDtypeStruct((2 * PAIRS, 3, padded, 128), jnp.float32)
    both, mine, other, mine_again, other_again = pl.pallas_call(
        functools.partial(pack_kernel, blocks_all),
        out_shape=[both_shape] + [group_shape] * 4,
        in_specs=[hbm, hbm],
        out_specs=[vmem] * 5,
        scratch_shapes=[
            pltpu.SMEM(p_cols.T.shape, jnp.int32),
            pltpu.VMEM(p_rows.shape, jnp.float32),
            pltpu.SemaphoreType.DMA((2,)),
        ],
        compiler_params=params,
        name="pack_window",
    )(in_hbm(p_cols.T), in_hbm(p_rows))

    pair_both = send(both, swap)
    pieces = [mine, pair_both]
    for shift in range(2, cols_axis):
        pieces.append(
            send(mine_again if shift % 2 == 0 else other_again, lambda row, col: (row, col ^ shift))
        )
    near = send(other, toward)
    k_split = pl.pallas_call(
        functools.partial(split_kernel, slots, total_rows),
        out_shape=jax.ShapeDtypeStruct((AGG, 3 * AGG + 1, fine, 128), jnp.bfloat16),
        in_specs=[hbm, hbm],
        out_specs=vmem,
        scratch_shapes=[
            pltpu.SMEM(k_cols.shape, jnp.int32),
            pltpu.VMEM((AGG, slots, fine, fine), jnp.float32),
            pltpu.SemaphoreType.DMA,
            pltpu.SemaphoreType.DMA((AGG,)),
        ],
        compiler_params=params,
        cost_estimate=pl.CostEstimate(flops=0, bytes_accessed=8_000_000, transcendentals=0),
        name="split_stiffness",
    )(in_hbm(k_cols), in_hbm(k_vals))

    k_split, pair_both = lax.optimization_barrier((k_split, pair_both))
    pieces[1] = pair_both
    pair_near = send(pair_both[:PAIRS], toward)

    stiff_shape = (2, AGG * fine, 128)
    place_shape = (PAIRS, 3, 2, padded, 128)
    p_shape = (AGG, fine, 256)
    stiff = pl.pallas_call(
        stiff_kernel,
        out_shape=jax.ShapeDtypeStruct((2, *stiff_shape), jnp.bfloat16),
        in_specs=[vmem] * 4,
        out_specs=vmem,
        scratch_shapes=[
            pltpu.VMEM((2, *place_shape), jnp.float32),
            pltpu.VMEM((2, *p_shape), jnp.bfloat16),
        ],
        compiler_params=params,
        cost_estimate=pl.CostEstimate(
            flops=1_000_000_000, bytes_accessed=3_000_000, transcendentals=0
        ),
        name="stiff_prolong",
    )(mine, other, pair_both, k_split)

    def part_scratch(windows):
        return [pltpu.VMEM((windows, PAIRS, cols_axis, padded, 128), jnp.bfloat16)] * 2

    edge, stiff_near = pl.pallas_call(
        functools.partial(edge_kernel, cols_axis, padded),
        out_shape=[
            jax.ShapeDtypeStruct((10, padded // 2, 2 * width), jnp.float32),
            jax.ShapeDtypeStruct(stiff_shape, jnp.bfloat16),
        ],
        in_specs=[vmem] * (4 + cols_axis),
        out_specs=[vmem] * 2,
        scratch_shapes=[pltpu.VMEM(place_shape, jnp.float32), pltpu.VMEM(p_shape, jnp.bfloat16)]
        + part_scratch(1),
        compiler_params=params,
        cost_estimate=pl.CostEstimate(
            flops=1_000_000_000, bytes_accessed=2_000_000, transcendentals=0
        ),
        name="edge_terms",
    )(k_split, stiff, *pieces, near, pair_near)
    from_edge = send(edge, away)

    band_shape = jax.ShapeDtypeStruct((5, padded, 2 * width), jnp.float32)
    own, for_pair = pl.pallas_call(
        functools.partial(inner_kernel, cols_axis, padded),
        out_shape=[band_shape] * 2,
        in_specs=[vmem] * (2 + cols_axis),
        out_specs=[vmem] * 2,
        scratch_shapes=part_scratch(2),
        compiler_params=params,
        cost_estimate=pl.CostEstimate(
            flops=500_000_000, bytes_accessed=1_000_000, transcendentals=0
        ),
        name="inner_terms",
    )(stiff, stiff_near, *pieces)
    from_pair = send(for_pair, swap)
    from_pair_edge = send(from_edge[5:], swap)

    coarse = pl.pallas_call(
        functools.partial(sum_kernel, padded),
        out_shape=jax.ShapeDtypeStruct((2, 7, padded, width), jnp.float32),
        in_specs=[vmem] * 4,
        out_specs=vmem,
        compiler_params=params,
        name="sum_terms",
    )(own, from_pair, from_edge, from_pair_edge)
    if padded != share:
        coarse = coarse.reshape(2, 7, padded, cols_axis, padded)[:, :, :share, :, :share]
        coarse = coarse.reshape(2, 7, share, cols_axis * share)
    return jnp.swapaxes(coarse, 2, 3)


def solution(mesh):
    placed = (
        P("row", None, None, None),
        P("row", None),
        P("row", None, None, "col"),
        P("row", None),
    )
    return jax.shard_map(
        functools.partial(body, rows_axis=mesh.shape["row"], cols_axis=mesh.shape["col"]),
        mesh=mesh,
        in_specs=placed,
        out_specs=P("row", None, None, "col"),
        check_vma=False,
    )
```

```python
import functools

import jax
import jax.numpy as jnp
from jax import lax
from jax.experimental import pallas as pl
from jax.experimental.pallas import tpu as pltpu
from jax.sharding import PartitionSpec as P

AGG = 8
PAIRS = AGG // 2


def split_high_low(value):
    high = value.astype(jnp.bfloat16)
    low = (value - high.astype(jnp.float32)).astype(jnp.bfloat16)
    return high, low


def pack_kernel(
    blocks_all, cols_hbm, p_hbm, both_ref, mine_ref, other_ref, mine_again, other_again,
    cols_ref, p_ref, sems,
):
    cols_copy = pltpu.make_async_copy(cols_hbm, cols_ref, sems.at[0])
    p_copy = pltpu.make_async_copy(p_hbm, p_ref, sems.at[1])
    cols_copy.start()
    p_copy.start()
    half = lax.axis_index("col") % 2
    first_agg = lax.axis_index("row") * 2
    blank = jnp.zeros(p_ref.shape[2:], jnp.float32)
    cols_copy.wait()
    p_copy.wait()
    for part, out_ref, again in ((0, mine_ref, mine_again), (1, other_ref, other_again)):
        group = half if part == 0 else 1 - half
        targets = []
        for window in range(3):
            target = first_agg + group - 1 + window
            targets.append(jnp.where((target >= 0) & (target < blocks_all), target, -2))
        for pair in range(PAIRS):
            rows = []
            for sub in range(2):
                row = group * AGG + 2 * pair + sub
                rows.append([(cols_ref[slot, row], p_ref[row, slot]) for slot in range(3)])
            for window, target in enumerate(targets):
                halves = []
                for slots in rows:
                    value = blank
                    for column, block in slots:
                        value = jnp.where(column == target, block, value)
                    halves.append(value)
                packed = jnp.concatenate(halves, axis=1)
                out_ref[pair, window] = packed
                again[pair, window] = packed
                both_ref[part * PAIRS + pair, window] = packed


def split_kernel(slots, total_rows, cols_hbm, k_hbm, out_ref, cols_ref, k_ref, cols_sem, sems):
    half = lax.axis_index("col") % 2
    first_row = lax.axis_index("row") * (2 * AGG) + half * AGG
    absent = 3 * AGG

    def k_copy(row):
        return pltpu.make_async_copy(k_hbm.at[half * AGG + row], k_ref.at[row], sems.at[row])

    cols_copy = pltpu.make_async_copy(cols_hbm, cols_ref, cols_sem)
    cols_copy.start()
    for row in range(AGG):
        k_copy(row).start()

    def one_blank(row, carry):
        for column in range(absent):
            out_ref[row, column] = jnp.zeros((64, 128), jnp.bfloat16)
        return carry

    lax.fori_loop(0, AGG, one_blank, 0)
    cols_copy.wait()

    def one_row(row, carry):
        k_copy(row).wait()
        for slot in range(slots):
            column = cols_ref[half * AGG + row, slot]
            present = (column >= 0) & (column < total_rows)
            place = jnp.where(present, column - first_row + AGG, absent)
            place = jnp.clip(place, 0, absent)
            out_ref[row, place] = jnp.concatenate(split_high_low(k_ref[row, slot]), axis=1)
        return carry

    lax.fori_loop(0, AGG, one_row, 0)


def transpose_blocks(sources, place_ref, p_ref):
    depth = place_ref.shape[1] * place_ref.shape[2] * place_ref.shape[3]
    for side, (source, first) in enumerate(sources):
        for pair in range(PAIRS):
            for window in range(3):
                place_ref[pair, window, side] = source[first + pair, window]
    for pair in range(PAIRS):
        turned = place_ref[pair].reshape(depth, 128).T
        for place, part in enumerate(split_high_low(turned)):
            for sub in range(2):
                p_ref[2 * pair + sub, :, 128 * place : 128 * place + depth] = part[
                    64 * sub : 64 * sub + 64
                ]


def stiff_product(step, k_ref, p_ref):
    rows = []
    blocks = []
    for row in range(AGG):
        rows.append(k_ref[:, step * AGG + row].reshape(AGG * 64, 128))
        blocks += [p_ref[row], p_ref[row]]
    total = jnp.dot(
        jnp.concatenate(rows, axis=1),
        jnp.concatenate(blocks, axis=0),
        preferred_element_type=jnp.float32,
    )
    return split_high_low(total[:, :128] + total[:, 128:])


def stiff_kernel(mine, other, pair_both, k_ref, out_ref, place_ref, p_ref):
    half = lax.axis_index("col") % 2
    for place, step, sources in (
        (0, 1, ((mine, 0), (pair_both, PAIRS))),
        (1, 2 - 2 * half, ((other, 0), (pair_both, 0))),
    ):
        transpose_blocks(sources, place_ref.at[place], p_ref.at[place])
        high, low = stiff_product(step, k_ref, p_ref.at[place])
        out_ref[place, 0] = high
        out_ref[place, 1] = low


def coarse_terms(stiffs, pieces, windows, share, high_ref, low_ref):
    count = len(pieces)
    width = count * share
    depth = 6 * share
    position = lax.axis_index("col")
    first_half = position % 2 == 0
    for place, window in enumerate(windows):
        for shift in range(count):
            first = PAIRS if shift == 1 else 0
            for pair in range(PAIRS):
                high, low = split_high_low(pieces[shift][first + pair, window])
                high_ref[place, pair, position ^ shift] = high
                low_ref[place, pair, position ^ shift] = low

    def rows_of(part):
        return jnp.concatenate(
            [
                jnp.concatenate(
                    [part[place, pair].reshape(width, 128) for pair in range(PAIRS)], axis=1
                )
                for place in range(len(windows))
            ],
            axis=0,
        )

    high, low = rows_of(high_ref), rows_of(low_ref)
    both = jnp.concatenate([high, low], axis=0)
    rows = len(windows) * width
    totals = []
    for stiff_high, stiff_low in stiffs:
        total = jnp.dot(both, stiff_high, preferred_element_type=jnp.float32)
        rest = jnp.dot(high, stiff_low, preferred_element_type=jnp.float32)
        totals.append(total[:rows] + total[rows:] + rest)
    mine, other, near = totals
    steps = (jnp.where(first_half, near, other), mine, jnp.where(first_half, other, near))
    terms = [[None] * 5 for _ in windows]
    for step, total in enumerate(steps):
        for place in range(len(windows)):
            turned = total[width * place : width * place + width].T[:depth]
            turned = turned.reshape(3, 2, share, width)
            for slot in range(3):
                before = terms[place][step + slot]
                terms[place][step + slot] = turned[slot] if before is None else before + turned[slot]
    return terms


def edge_kernel(count, share, k_ref, stiff, *refs):
    pieces = [*refs[:2], *refs[2:count][::-1]]
    near, pair_near, edge_ref, near_ref, place_ref, p_ref, high_ref, low_ref = refs[count:]
    half = lax.axis_index("col") % 2
    transpose_blocks(((near, 0), (pair_near, 0)), place_ref, p_ref)
    high, low = stiff_product(2 * half, k_ref, p_ref)
    near_ref[0] = high
    near_ref[1] = low
    stiffs = [(stiff[place, 0], stiff[place, 1]) for place in range(2)] + [(high, low)]
    (terms,) = coarse_terms(stiffs, pieces, (2 * half,), share, high_ref, low_ref)
    for slot in range(5):
        for side in range(2):
            term = terms[slot][side]
            folded = jnp.concatenate([term[: share // 2], term[share // 2 :]], axis=1)
            edge_ref[5 * side + slot] = folded


def inner_kernel(count, share, stiff, stiff_near, *refs):
    pieces = [*refs[:2], *refs[2:count][::-1]]
    own_ref, pair_ref, high_ref, low_ref = refs[count:]
    half = lax.axis_index("col") % 2
    width = count * share
    stiffs = [(stiff[place, 0], stiff[place, 1]) for place in range(2)]
    stiffs.append((stiff_near[0], stiff_near[1]))
    windows = (1 - half, 2 - half)
    lower, upper = coarse_terms(stiffs, pieces, windows, share, high_ref, low_ref)
    for side, ref in ((0, own_ref), (1, pair_ref)):
        for slot in range(5):
            ref[slot] = jnp.concatenate([lower[slot][side], upper[slot][side]], axis=1)


def sum_kernel(share, own, from_pair, from_edge, from_pair_edge, out_ref):
    half = lax.axis_index("col") % 2
    width = own.shape[2] // 2

    def unfold(folded):
        return jnp.concatenate([folded[:, :width], folded[:, width:]], axis=0)

    def write(lower, upper, before, after):
        for offset in range(7):
            first = [lower[offset - 1][:, :width]] if 1 <= offset < 6 else []
            first += [upper[offset - 2][:, :width]] if 2 <= offset else []
            first += [unfold(before[offset])] if offset < 5 else []
            out_ref[0, offset] = sum(first[1:], first[0])
            second = [lower[offset][:, width:]] if offset < 5 else []
            second += [upper[offset - 1][:, width:]] if 1 <= offset < 6 else []
            second += [unfold(after[offset - 2])] if 2 <= offset else []
            out_ref[1, offset] = sum(second[1:], second[0])

    @pl.when(half == 0)
    def _():
        write(own, from_pair, from_pair_edge, from_edge)

    @pl.when(half == 1)
    def _():
        write(from_pair, own, from_edge, from_pair_edge)


def body(k_vals, k_cols, p_vals, p_cols, *, rows_axis, cols_axis):
    own_rows, slots, fine, _ = k_vals.shape
    share = p_vals.shape[3]
    padded = -(-share // 16) * 16
    total_rows = own_rows * rows_axis
    blocks_all = total_rows // AGG
    width = cols_axis * padded
    vmem = pl.BlockSpec(memory_space=pltpu.VMEM)
    hbm = pl.BlockSpec(memory_space=pltpu.HBM)
    params = pltpu.CompilerParams(vmem_limit_bytes=24 * 1024 * 1024)

    def in_hbm(value):
        return pltpu.with_memory_space_constraint(value, pltpu.HBM)

    def send(value, target):
        perm = []
        for row in range(rows_axis):
            for col in range(cols_axis):
                to_row, to_col = target(row, col)
                perm.append((row * cols_axis + col, to_row * cols_axis + to_col))
        return lax.ppermute(value, ("row", "col"), perm)

    def toward(row, col):
        return (row + (1 if col % 2 == 0 else -1)) % rows_axis, col

    def away(row, col):
        to_row = row - (1 if col % 2 == 0 else -1)
        return (to_row, col) if 0 <= to_row < rows_axis else swap(row, col)

    def swap(row, col):
        return row, col ^ 1

    p_rows = jnp.swapaxes(p_vals, 2, 3)
    if padded != share:
        p_rows = jnp.pad(p_rows, ((0, 0), (0, 0), (0, padded - share), (0, 0)))
    group_shape = jax.ShapeDtypeStruct((PAIRS, 3, padded, 128), jnp.float32)
    both_shape = jax.ShapeDtypeStruct((2 * PAIRS, 3, padded, 128), jnp.float32)
    both, mine, other, mine_again, other_again = pl.pallas_call(
        functools.partial(pack_kernel, blocks_all),
        out_shape=[both_shape] + [group_shape] * 4,
        in_specs=[hbm, hbm],
        out_specs=[vmem] * 5,
        scratch_shapes=[
            pltpu.SMEM(p_cols.T.shape, jnp.int32),
            pltpu.VMEM(p_rows.shape, jnp.float32),
            pltpu.SemaphoreType.DMA((2,)),
        ],
        compiler_params=params,
        name="pack_window",
    )(in_hbm(p_cols.T), in_hbm(p_rows))

    pair_both = send(both, swap)
    pieces = [mine, pair_both]
    for shift in range(2, cols_axis):
        pieces.append(
            send(mine_again if shift % 2 == 0 else other_again, lambda row, col: (row, col ^ shift))
        )
    near = send(other, toward)
    k_split = pl.pallas_call(
        functools.partial(split_kernel, slots, total_rows),
        out_shape=jax.ShapeDtypeStruct((AGG, 3 * AGG + 1, fine, 128), jnp.bfloat16),
        in_specs=[hbm, hbm],
        out_specs=vmem,
        scratch_shapes=[
            pltpu.SMEM(k_cols.shape, jnp.int32),
            pltpu.VMEM((AGG, slots, fine, fine), jnp.float32),
            pltpu.SemaphoreType.DMA,
            pltpu.SemaphoreType.DMA((AGG,)),
        ],
        compiler_params=params,
        cost_estimate=pl.CostEstimate(flops=0, bytes_accessed=8_000_000, transcendentals=0),
        name="split_stiffness",
    )(in_hbm(k_cols), in_hbm(k_vals))

    k_split, pair_both = lax.optimization_barrier((k_split, pair_both))
    pieces[1] = pair_both
    pair_near = send(pair_both[:PAIRS], toward)
    pieces = [*pieces[:2], *pieces[2:][::-1]]

    stiff_shape = (2, AGG * fine, 128)
    place_shape = (PAIRS, 3, 2, padded, 128)
    p_shape = (AGG, fine, 256)
    stiff = pl.pallas_call(
        stiff_kernel,
        out_shape=jax.ShapeDtypeStruct((2, *stiff_shape), jnp.bfloat16),
        in_specs=[vmem] * 4,
        out_specs=vmem,
        scratch_shapes=[
            pltpu.VMEM((2, *place_shape), jnp.float32),
            pltpu.VMEM((2, *p_shape), jnp.bfloat16),
        ],
        compiler_params=params,
        cost_estimate=pl.CostEstimate(
            flops=1_000_000_000, bytes_accessed=3_000_000, transcendentals=0
        ),
        name="stiff_prolong",
    )(mine, other, pair_both, k_split)

    def part_scratch(windows):
        return [pltpu.VMEM((windows, PAIRS, cols_axis, padded, 128), jnp.bfloat16)] * 2

    edge, stiff_near = pl.pallas_call(
        functools.partial(edge_kernel, cols_axis, padded),
        out_shape=[
            jax.ShapeDtypeStruct((10, padded // 2, 2 * width), jnp.float32),
            jax.ShapeDtypeStruct(stiff_shape, jnp.bfloat16),
        ],
        in_specs=[vmem] * (4 + cols_axis),
        out_specs=[vmem] * 2,
        scratch_shapes=[pltpu.VMEM(place_shape, jnp.float32), pltpu.VMEM(p_shape, jnp.bfloat16)]
        + part_scratch(1),
        compiler_params=params,
        cost_estimate=pl.CostEstimate(
            flops=1_000_000_000, bytes_accessed=2_000_000, transcendentals=0
        ),
        name="edge_terms",
    )(k_split, stiff, *pieces, near, pair_near)
    from_edge = send(edge, away)

    band_shape = jax.ShapeDtypeStruct((5, padded, 2 * width), jnp.float32)
    own, for_pair = pl.pallas_call(
        functools.partial(inner_kernel, cols_axis, padded),
        out_shape=[band_shape] * 2,
        in_specs=[vmem] * (2 + cols_axis),
        out_specs=[vmem] * 2,
        scratch_shapes=part_scratch(2),
        compiler_params=params,
        cost_estimate=pl.CostEstimate(
            flops=500_000_000, bytes_accessed=1_000_000, transcendentals=0
        ),
        name="inner_terms",
    )(stiff, stiff_near, *pieces)
    from_pair = send(for_pair, swap)
    from_pair_edge = send(from_edge[5:], swap)

    coarse = pl.pallas_call(
        functools.partial(sum_kernel, padded),
        out_shape=jax.ShapeDtypeStruct((2, 7, padded, width), jnp.float32),
        in_specs=[vmem] * 4,
        out_specs=vmem,
        compiler_params=params,
        name="sum_terms",
    )(own, from_pair, from_edge, from_pair_edge)
    if padded != share:
        coarse = coarse.reshape(2, 7, padded, cols_axis, padded)[:, :, :share, :, :share]
        coarse = coarse.reshape(2, 7, share, cols_axis * share)
    return jnp.swapaxes(coarse, 2, 3)


def solution(mesh):
    placed = (
        P("row", None, None, None),
        P("row", None),
        P("row", None, None, "col"),
        P("row", None),
    )
    return jax.shard_map(
        functools.partial(body, rows_axis=mesh.shape["row"], cols_axis=mesh.shape["col"]),
        mesh=mesh,
        in_specs=placed,
        out_specs=P("row", None, None, "col"),
        check_vma=False,
    )
```

```python
import functools

import jax
import jax.numpy as jnp
from jax import lax
from jax.experimental import pallas as pl
from jax.experimental.pallas import tpu as pltpu
from jax.sharding import PartitionSpec as P

AGG = 8
PAIRS = AGG // 2


def split_high_low(value):
    high = value.astype(jnp.bfloat16)
    low = (value - high.astype(jnp.float32)).astype(jnp.bfloat16)
    return high, low


def pack_kernel(
    blocks_all, cols_hbm, p_hbm, both_ref, mine_ref, other_ref, mine_again, other_again,
    cols_ref, p_ref, sems,
):
    cols_copy = pltpu.make_async_copy(cols_hbm, cols_ref, sems.at[0])
    p_copy = pltpu.make_async_copy(p_hbm, p_ref, sems.at[1])
    cols_copy.start()
    p_copy.start()
    half = lax.axis_index("col") % 2
    first_agg = lax.axis_index("row") * 2
    blank = jnp.zeros(p_ref.shape[2:], jnp.float32)
    cols_copy.wait()
    p_copy.wait()
    for part, out_ref, again in ((0, mine_ref, mine_again), (1, other_ref, other_again)):
        group = half if part == 0 else 1 - half
        targets = []
        for window in range(3):
            target = first_agg + group - 1 + window
            targets.append(jnp.where((target >= 0) & (target < blocks_all), target, -2))
        for pair in range(PAIRS):
            rows = []
            for sub in range(2):
                row = group * AGG + 2 * pair + sub
                rows.append([(cols_ref[slot, row], p_ref[row, slot]) for slot in range(3)])
            for window, target in enumerate(targets):
                halves = []
                for slots in rows:
                    value = blank
                    for column, block in slots:
                        value = jnp.where(column == target, block, value)
                    halves.append(value)
                packed = jnp.concatenate(halves, axis=1)
                out_ref[pair, window] = packed
                again[pair, window] = packed
                both_ref[part * PAIRS + pair, window] = packed


def split_kernel(slots, total_rows, cols_hbm, k_hbm, out_ref, cols_ref, k_ref, cols_sem, sems):
    half = lax.axis_index("col") % 2
    first_row = lax.axis_index("row") * (2 * AGG) + half * AGG
    absent = 3 * AGG

    def k_copy(row):
        return pltpu.make_async_copy(k_hbm.at[half * AGG + row], k_ref.at[row], sems.at[row])

    cols_copy = pltpu.make_async_copy(cols_hbm, cols_ref, cols_sem)
    cols_copy.start()
    for row in range(AGG):
        k_copy(row).start()

    def one_blank(row, carry):
        for column in range(absent):
            out_ref[row, column] = jnp.zeros((64, 128), jnp.bfloat16)
        return carry

    lax.fori_loop(0, AGG, one_blank, 0)
    cols_copy.wait()

    def one_row(row, carry):
        k_copy(row).wait()
        for slot in range(slots):
            column = cols_ref[half * AGG + row, slot]
            present = (column >= 0) & (column < total_rows)
            place = jnp.where(present, column - first_row + AGG, absent)
            place = jnp.clip(place, 0, absent)
            out_ref[row, place] = jnp.concatenate(split_high_low(k_ref[row, slot]), axis=1)
        return carry

    lax.fori_loop(0, AGG, one_row, 0)


def transpose_blocks(sources, p_ref):
    for pair in range(PAIRS):
        block = jnp.concatenate(
            [source[first + pair, window] for window in range(3) for source, first in sources],
            axis=0,
        )
        depth = block.shape[0]
        for place, part in enumerate(split_high_low(block.T)):
            for sub in range(2):
                p_ref[2 * pair + sub, :, 128 * place : 128 * place + depth] = part[
                    64 * sub : 64 * sub + 64
                ]


def stiff_product(step, k_ref, p_ref):
    rows = []
    blocks = []
    for row in range(AGG):
        rows.append(k_ref[:, step * AGG + row].reshape(AGG * 64, 128))
        blocks += [p_ref[row], p_ref[row]]
    total = jnp.dot(
        jnp.concatenate(rows, axis=1),
        jnp.concatenate(blocks, axis=0),
        preferred_element_type=jnp.float32,
    )
    return jnp.concatenate(split_high_low(total[:, :128] + total[:, 128:]), axis=1)


def stiff_kernel(mine, other, pair_both, k_ref, out_ref, p_ref):
    half = lax.axis_index("col") % 2
    for place, step, sources in (
        (0, 1, ((mine, 0), (pair_both, PAIRS))),
        (1, 2 - 2 * half, ((other, 0), (pair_both, 0))),
    ):
        transpose_blocks(sources, p_ref.at[place])
        out_ref[place] = stiff_product(step, k_ref, p_ref.at[place])


def coarse_terms(stiffs, pieces, windows, share, high_ref, low_ref):
    count = len(pieces)
    width = count * share
    depth = 6 * share
    position = lax.axis_index("col")
    first_half = position % 2 == 0
    for place, window in enumerate(windows):
        for shift in range(count):
            first = PAIRS if shift == 1 else 0
            for pair in range(PAIRS):
                high, low = split_high_low(pieces[shift][first + pair, window])
                high_ref[place, pair, position ^ shift] = high
                low_ref[place, pair, position ^ shift] = low

    def rows_of(part):
        return jnp.concatenate(
            [
                jnp.concatenate(
                    [part[place, pair].reshape(width, 128) for pair in range(PAIRS)], axis=1
                )
                for place in range(len(windows))
            ],
            axis=0,
        )

    high, low = rows_of(high_ref), rows_of(low_ref)
    both = jnp.concatenate([high, low], axis=0)
    rows = len(windows) * width
    totals = []
    for stiff in stiffs:
        total = jnp.dot(both, stiff, preferred_element_type=jnp.float32)
        total = total[:rows] + total[rows:]
        totals.append(total[:, :128] + total[:, 128:])
    mine, other, near = totals
    steps = (jnp.where(first_half, near, other), mine, jnp.where(first_half, other, near))
    terms = [[None] * 5 for _ in windows]
    for step, total in enumerate(steps):
        for place in range(len(windows)):
            turned = total[width * place : width * place + width].T[:depth]
            turned = turned.reshape(3, 2, share, width)
            for slot in range(3):
                before = terms[place][step + slot]
                terms[place][step + slot] = turned[slot] if before is None else before + turned[slot]
    return terms


def edge_kernel(count, share, k_ref, stiff, *refs):
    pieces = refs[:count]
    near, pair_near, edge_ref, near_ref, p_ref, high_ref, low_ref = refs[count:]
    half = lax.axis_index("col") % 2
    transpose_blocks(((near, 0), (pair_near, 0)), p_ref)
    stiff_near = stiff_product(2 * half, k_ref, p_ref)
    near_ref[...] = stiff_near
    stiffs = [stiff[0], stiff[1], stiff_near]
    (terms,) = coarse_terms(stiffs, pieces, (2 * half,), share, high_ref, low_ref)
    for slot in range(5):
        for side in range(2):
            term = terms[slot][side]
            folded = jnp.concatenate([term[: share // 2], term[share // 2 :]], axis=1)
            edge_ref[5 * side + slot] = folded


def inner_kernel(count, share, stiff, stiff_near, *refs):
    pieces = refs[:count]
    own_ref, pair_ref, high_ref, low_ref = refs[count:]
    half = lax.axis_index("col") % 2
    width = count * share
    stiffs = [stiff[0], stiff[1], stiff_near[...]]
    windows = (1 - half, 2 - half)
    lower, upper = coarse_terms(stiffs, pieces, windows, share, high_ref, low_ref)
    for side, ref in ((0, own_ref), (1, pair_ref)):
        for slot in range(5):
            ref[slot] = jnp.concatenate([lower[slot][side], upper[slot][side]], axis=1)


def sum_kernel(share, own, from_pair, from_edge, from_pair_edge, out_ref):
    half = lax.axis_index("col") % 2
    width = own.shape[2] // 2

    def unfold(folded):
        return jnp.concatenate([folded[:, :width], folded[:, width:]], axis=0)

    def write(lower, upper, before, after):
        for offset in range(7):
            first = [lower[offset - 1][:, :width]] if 1 <= offset < 6 else []
            first += [upper[offset - 2][:, :width]] if 2 <= offset else []
            first += [unfold(before[offset])] if offset < 5 else []
            out_ref[0, offset] = sum(first[1:], first[0])
            second = [lower[offset][:, width:]] if offset < 5 else []
            second += [upper[offset - 1][:, width:]] if 1 <= offset < 6 else []
            second += [unfold(after[offset - 2])] if 2 <= offset else []
            out_ref[1, offset] = sum(second[1:], second[0])

    @pl.when(half == 0)
    def _():
        write(own, from_pair, from_pair_edge, from_edge)

    @pl.when(half == 1)
    def _():
        write(from_pair, own, from_edge, from_pair_edge)


def body(k_vals, k_cols, p_vals, p_cols, *, rows_axis, cols_axis):
    own_rows, slots, fine, _ = k_vals.shape
    share = p_vals.shape[3]
    padded = -(-share // 16) * 16
    total_rows = own_rows * rows_axis
    blocks_all = total_rows // AGG
    width = cols_axis * padded
    vmem = pl.BlockSpec(memory_space=pltpu.VMEM)
    hbm = pl.BlockSpec(memory_space=pltpu.HBM)
    params = pltpu.CompilerParams(vmem_limit_bytes=24 * 1024 * 1024)

    def in_hbm(value):
        return pltpu.with_memory_space_constraint(value, pltpu.HBM)

    def send(value, target):
        perm = []
        for row in range(rows_axis):
            for col in range(cols_axis):
                to_row, to_col = target(row, col)
                perm.append((row * cols_axis + col, to_row * cols_axis + to_col))
        return lax.ppermute(value, ("row", "col"), perm)

    def toward(row, col):
        return (row + (1 if col % 2 == 0 else -1)) % rows_axis, col

    def away(row, col):
        to_row = row - (1 if col % 2 == 0 else -1)
        return (to_row, col) if 0 <= to_row < rows_axis else swap(row, col)

    def swap(row, col):
        return row, col ^ 1

    p_rows = jnp.swapaxes(p_vals, 2, 3)
    if padded != share:
        p_rows = jnp.pad(p_rows, ((0, 0), (0, 0), (0, padded - share), (0, 0)))
    group_shape = jax.ShapeDtypeStruct((PAIRS, 3, padded, 128), jnp.float32)
    both_shape = jax.ShapeDtypeStruct((2 * PAIRS, 3, padded, 128), jnp.float32)
    both, mine, other, mine_again, other_again = pl.pallas_call(
        functools.partial(pack_kernel, blocks_all),
        out_shape=[both_shape] + [group_shape] * 4,
        in_specs=[hbm, hbm],
        out_specs=[vmem] * 5,
        scratch_shapes=[
            pltpu.SMEM(p_cols.T.shape, jnp.int32),
            pltpu.VMEM(p_rows.shape, jnp.float32),
            pltpu.SemaphoreType.DMA((2,)),
        ],
        compiler_params=params,
        name="pack_window",
    )(in_hbm(p_cols.T), in_hbm(p_rows))

    pair_both = send(both, swap)
    pieces = [mine, pair_both]
    for shift in range(2, cols_axis):
        pieces.append(
            send(mine_again if shift % 2 == 0 else other_again, lambda row, col: (row, col ^ shift))
        )
    near = send(other, toward)
    k_split = pl.pallas_call(
        functools.partial(split_kernel, slots, total_rows),
        out_shape=jax.ShapeDtypeStruct((AGG, 3 * AGG + 1, fine, 128), jnp.bfloat16),
        in_specs=[hbm, hbm],
        out_specs=vmem,
        scratch_shapes=[
            pltpu.SMEM(k_cols.shape, jnp.int32),
            pltpu.VMEM((AGG, slots, fine, fine), jnp.float32),
            pltpu.SemaphoreType.DMA,
            pltpu.SemaphoreType.DMA((AGG,)),
        ],
        compiler_params=params,
        cost_estimate=pl.CostEstimate(flops=0, bytes_accessed=8_000_000, transcendentals=0),
        name="split_stiffness",
    )(in_hbm(k_cols), in_hbm(k_vals))

    k_split, pair_both = lax.optimization_barrier((k_split, pair_both))
    pieces[1] = pair_both
    pair_near = send(pair_both[:PAIRS], toward)

    stiff_shape = (AGG * fine, 256)
    p_shape = (AGG, fine, 256)
    stiff = pl.pallas_call(
        stiff_kernel,
        out_shape=jax.ShapeDtypeStruct((2, *stiff_shape), jnp.bfloat16),
        in_specs=[vmem] * 4,
        out_specs=vmem,
        scratch_shapes=[pltpu.VMEM((2, *p_shape), jnp.bfloat16)],
        compiler_params=params,
        cost_estimate=pl.CostEstimate(
            flops=1_000_000_000, bytes_accessed=3_000_000, transcendentals=0
        ),
        name="stiff_prolong",
    )(mine, other, pair_both, k_split)

    def part_scratch(windows):
        return [pltpu.VMEM((windows, PAIRS, cols_axis, padded, 128), jnp.bfloat16)] * 2

    edge, stiff_near = pl.pallas_call(
        functools.partial(edge_kernel, cols_axis, padded),
        out_shape=[
            jax.ShapeDtypeStruct((10, padded // 2, 2 * width), jnp.float32),
            jax.ShapeDtypeStruct(stiff_shape, jnp.bfloat16),
        ],
        in_specs=[vmem] * (4 + cols_axis),
        out_specs=[vmem] * 2,
        scratch_shapes=[pltpu.VMEM(p_shape, jnp.bfloat16)]
        + part_scratch(1),
        compiler_params=params,
        cost_estimate=pl.CostEstimate(
            flops=1_000_000_000, bytes_accessed=2_000_000, transcendentals=0
        ),
        name="edge_terms",
    )(k_split, stiff, *pieces, near, pair_near)
    from_edge = send(edge, away)

    band_shape = jax.ShapeDtypeStruct((5, padded, 2 * width), jnp.float32)
    own, for_pair = pl.pallas_call(
        functools.partial(inner_kernel, cols_axis, padded),
        out_shape=[band_shape] * 2,
        in_specs=[vmem] * (2 + cols_axis),
        out_specs=[vmem] * 2,
        scratch_shapes=part_scratch(2),
        compiler_params=params,
        cost_estimate=pl.CostEstimate(
            flops=500_000_000, bytes_accessed=1_000_000, transcendentals=0
        ),
        name="inner_terms",
    )(stiff, stiff_near, *pieces)
    from_pair = send(for_pair, swap)
    from_pair_edge = send(from_edge[5:], swap)

    coarse = pl.pallas_call(
        functools.partial(sum_kernel, padded),
        out_shape=jax.ShapeDtypeStruct((2, 7, padded, width), jnp.float32),
        in_specs=[vmem] * 4,
        out_specs=vmem,
        compiler_params=params,
        name="sum_terms",
    )(own, from_pair, from_edge, from_pair_edge)
    if padded != share:
        coarse = coarse.reshape(2, 7, padded, cols_axis, padded)[:, :, :share, :, :share]
        coarse = coarse.reshape(2, 7, share, cols_axis * share)
    return jnp.swapaxes(coarse, 2, 3)


def solution(mesh):
    placed = (
        P("row", None, None, None),
        P("row", None),
        P("row", None, None, "col"),
        P("row", None),
    )
    return jax.shard_map(
        functools.partial(body, rows_axis=mesh.shape["row"], cols_axis=mesh.shape["col"]),
        mesh=mesh,
        in_specs=placed,
        out_specs=P("row", None, None, "col"),
        check_vma=False,
    )
```

```python
import functools

import jax
import jax.numpy as jnp
from jax import lax
from jax.experimental import pallas as pl
from jax.experimental.pallas import tpu as pltpu
from jax.sharding import PartitionSpec as P

AGG = 8
PAIRS = AGG // 2


def split_high_low(value):
    high = value.astype(jnp.bfloat16)
    low = (value - high.astype(jnp.float32)).astype(jnp.bfloat16)
    return high, low


def pack_kernel(
    blocks_all, cols_hbm, p_hbm, mine_ref, other_ref, mine_again, other_again,
    cols_ref, p_ref, sems,
):
    cols_copy = pltpu.make_async_copy(cols_hbm, cols_ref, sems.at[0])
    p_copy = pltpu.make_async_copy(p_hbm, p_ref, sems.at[1])
    cols_copy.start()
    p_copy.start()
    half = lax.axis_index("col") % 2
    first_agg = lax.axis_index("row") * 2
    blank = jnp.zeros(p_ref.shape[2:], jnp.float32)
    cols_copy.wait()
    p_copy.wait()
    for part, out_ref, again in ((0, mine_ref, mine_again), (1, other_ref, other_again)):
        group = half if part == 0 else 1 - half
        targets = []
        for window in range(3):
            target = first_agg + group - 1 + window
            targets.append(jnp.where((target >= 0) & (target < blocks_all), target, -2))
        for pair in range(PAIRS):
            rows = []
            for sub in range(2):
                row = group * AGG + 2 * pair + sub
                rows.append([(cols_ref[slot, row], p_ref[row, slot]) for slot in range(3)])
            for window, target in enumerate(targets):
                halves = []
                for slots in rows:
                    value = blank
                    for column, block in slots:
                        value = jnp.where(column == target, block, value)
                    halves.append(value)
                packed = jnp.concatenate(halves, axis=1)
                out_ref[pair, window] = packed
                again[pair, window] = packed


def split_kernel(slots, total_rows, cols_hbm, k_hbm, out_ref, cols_ref, k_ref, cols_sem, sems):
    half = lax.axis_index("col") % 2
    first_row = lax.axis_index("row") * (2 * AGG) + half * AGG
    absent = 3 * AGG

    def k_copy(row):
        return pltpu.make_async_copy(k_hbm.at[half * AGG + row], k_ref.at[row], sems.at[row])

    cols_copy = pltpu.make_async_copy(cols_hbm, cols_ref, cols_sem)
    cols_copy.start()
    for row in range(AGG):
        k_copy(row).start()

    def one_blank(row, carry):
        for column in range(absent):
            out_ref[row, column] = jnp.zeros((64, 128), jnp.bfloat16)
        return carry

    lax.fori_loop(0, AGG, one_blank, 0)
    cols_copy.wait()

    def one_row(row, carry):
        k_copy(row).wait()
        for slot in range(slots):
            column = cols_ref[half * AGG + row, slot]
            present = (column >= 0) & (column < total_rows)
            place = jnp.where(present, column - first_row + AGG, absent)
            place = jnp.clip(place, 0, absent)
            out_ref[row, place] = jnp.concatenate(split_high_low(k_ref[row, slot]), axis=1)
        return carry

    lax.fori_loop(0, AGG, one_row, 0)


def transpose_blocks(sources, p_ref):
    for pair in range(PAIRS):
        block = jnp.concatenate(
            [source[pair, window] for window in range(3) for source in sources],
            axis=0,
        )
        depth = block.shape[0]
        for place, part in enumerate(split_high_low(block.T)):
            for sub in range(2):
                p_ref[2 * pair + sub, :, 128 * place : 128 * place + depth] = part[
                    64 * sub : 64 * sub + 64
                ]


def stiff_product(step, k_ref, p_ref):
    rows = []
    blocks = []
    for row in range(AGG):
        rows.append(k_ref[:, step * AGG + row].reshape(AGG * 64, 128))
        blocks += [p_ref[row], p_ref[row]]
    total = jnp.dot(
        jnp.concatenate(rows, axis=1),
        jnp.concatenate(blocks, axis=0),
        preferred_element_type=jnp.float32,
    )
    return jnp.concatenate(split_high_low(total[:, :128] + total[:, 128:]), axis=1)


def stiff_kernel(other, pair_other, k_ref, out_ref, p_ref):
    half = lax.axis_index("col") % 2
    transpose_blocks((other, pair_other), p_ref)
    out_ref[...] = stiff_product(2 - 2 * half, k_ref, p_ref)


def coarse_terms(stiffs, pieces, windows, share, high_ref, low_ref):
    count = len(pieces)
    width = count * share
    depth = 6 * share
    position = lax.axis_index("col")
    first_half = position % 2 == 0
    for place, window in enumerate(windows):
        for shift in range(count):
            for pair in range(PAIRS):
                high, low = split_high_low(pieces[shift][pair, window])
                high_ref[place, pair, position ^ shift] = high
                low_ref[place, pair, position ^ shift] = low

    def rows_of(part):
        return jnp.concatenate(
            [
                jnp.concatenate(
                    [part[place, pair].reshape(width, 128) for pair in range(PAIRS)], axis=1
                )
                for place in range(len(windows))
            ],
            axis=0,
        )

    high, low = rows_of(high_ref), rows_of(low_ref)
    both = jnp.concatenate([high, low], axis=0)
    rows = len(windows) * width
    totals = []
    for stiff in stiffs:
        total = jnp.dot(both, stiff, preferred_element_type=jnp.float32)
        total = total[:rows] + total[rows:]
        totals.append(total[:, :128] + total[:, 128:])
    mine, other, near = totals
    steps = (jnp.where(first_half, near, other), mine, jnp.where(first_half, other, near))
    terms = [[None] * 5 for _ in windows]
    for step, total in enumerate(steps):
        for place in range(len(windows)):
            turned = total[width * place : width * place + width].T[:depth]
            turned = turned.reshape(3, 2, share, width)
            for slot in range(3):
                before = terms[place][step + slot]
                terms[place][step + slot] = turned[slot] if before is None else before + turned[slot]
    return terms


def edge_kernel(count, share, k_ref, stiff_other, *refs):
    mine = refs[0]
    far = refs[1 : count - 1]
    near, pair_near, pair_mine = refs[count - 1 : count + 2]
    edge_ref, stiff_ref, p_ref, high_ref, low_ref = refs[count + 2 :]
    half = lax.axis_index("col") % 2
    stiffs = []
    for place, step, sources in (
        (0, 1, (mine, pair_mine)),
        (1, 2 * half, (near, pair_near)),
    ):
        transpose_blocks(sources, p_ref.at[place])
        stiffs.append(stiff_product(step, k_ref, p_ref.at[place]))
        stiff_ref[place] = stiffs[place]
    stiffs.insert(1, stiff_other[...])
    pieces = [mine, pair_mine, *far]
    (terms,) = coarse_terms(stiffs, pieces, (2 * half,), share, high_ref, low_ref)
    for slot in range(5):
        for side in range(2):
            term = terms[slot][side]
            folded = jnp.concatenate([term[: share // 2], term[share // 2 :]], axis=1)
            edge_ref[5 * side + slot] = folded


def inner_kernel(count, share, stiff_other, stiff, *refs):
    pieces = refs[:count]
    own_ref, pair_ref, high_ref, low_ref = refs[count:]
    half = lax.axis_index("col") % 2
    width = count * share
    stiffs = [stiff[0], stiff_other[...], stiff[1]]
    windows = (1 - half, 2 - half)
    lower, upper = coarse_terms(stiffs, pieces, windows, share, high_ref, low_ref)
    for side, ref in ((0, own_ref), (1, pair_ref)):
        for slot in range(5):
            ref[slot] = jnp.concatenate([lower[slot][side], upper[slot][side]], axis=1)


def sum_kernel(share, own, from_pair, from_edge, from_pair_edge, out_ref):
    half = lax.axis_index("col") % 2
    width = own.shape[2] // 2

    def unfold(folded):
        return jnp.concatenate([folded[:, :width], folded[:, width:]], axis=0)

    def write(lower, upper, before, after):
        for offset in range(7):
            first = [lower[offset - 1][:, :width]] if 1 <= offset < 6 else []
            first += [upper[offset - 2][:, :width]] if 2 <= offset else []
            first += [unfold(before[offset])] if offset < 5 else []
            out_ref[0, offset] = sum(first[1:], first[0])
            second = [lower[offset][:, width:]] if offset < 5 else []
            second += [upper[offset - 1][:, width:]] if 1 <= offset < 6 else []
            second += [unfold(after[offset - 2])] if 2 <= offset else []
            out_ref[1, offset] = sum(second[1:], second[0])

    @pl.when(half == 0)
    def _():
        write(own, from_pair, from_pair_edge, from_edge)

    @pl.when(half == 1)
    def _():
        write(from_pair, own, from_edge, from_pair_edge)


def body(k_vals, k_cols, p_vals, p_cols, *, rows_axis, cols_axis):
    own_rows, slots, fine, _ = k_vals.shape
    share = p_vals.shape[3]
    padded = -(-share // 16) * 16
    total_rows = own_rows * rows_axis
    blocks_all = total_rows // AGG
    width = cols_axis * padded
    vmem = pl.BlockSpec(memory_space=pltpu.VMEM)
    hbm = pl.BlockSpec(memory_space=pltpu.HBM)
    params = pltpu.CompilerParams(vmem_limit_bytes=24 * 1024 * 1024)

    def in_hbm(value):
        return pltpu.with_memory_space_constraint(value, pltpu.HBM)

    def send(value, target):
        perm = []
        for row in range(rows_axis):
            for col in range(cols_axis):
                to_row, to_col = target(row, col)
                perm.append((row * cols_axis + col, to_row * cols_axis + to_col))
        return lax.ppermute(value, ("row", "col"), perm)

    def toward(row, col):
        return (row + (1 if col % 2 == 0 else -1)) % rows_axis, col

    def away(row, col):
        to_row = row - (1 if col % 2 == 0 else -1)
        return (to_row, col) if 0 <= to_row < rows_axis else swap(row, col)

    def swap(row, col):
        return row, col ^ 1

    p_rows = jnp.swapaxes(p_vals, 2, 3)
    if padded != share:
        p_rows = jnp.pad(p_rows, ((0, 0), (0, 0), (0, padded - share), (0, 0)))
    group_shape = jax.ShapeDtypeStruct((PAIRS, 3, padded, 128), jnp.float32)
    mine, other, mine_again, other_again = pl.pallas_call(
        functools.partial(pack_kernel, blocks_all),
        out_shape=[group_shape] * 4,
        in_specs=[hbm, hbm],
        out_specs=[vmem] * 4,
        scratch_shapes=[
            pltpu.SMEM(p_cols.T.shape, jnp.int32),
            pltpu.VMEM(p_rows.shape, jnp.float32),
            pltpu.SemaphoreType.DMA((2,)),
        ],
        compiler_params=params,
        name="pack_window",
    )(in_hbm(p_cols.T), in_hbm(p_rows))

    pair_other = send(mine, swap)
    far = []
    for shift in range(2, cols_axis):
        far.append(
            send(mine_again if shift % 2 == 0 else other_again, lambda row, col: (row, col ^ shift))
        )
    near = send(other, toward)
    k_split = pl.pallas_call(
        functools.partial(split_kernel, slots, total_rows),
        out_shape=jax.ShapeDtypeStruct((AGG, 3 * AGG + 1, fine, 128), jnp.bfloat16),
        in_specs=[hbm, hbm],
        out_specs=vmem,
        scratch_shapes=[
            pltpu.SMEM(k_cols.shape, jnp.int32),
            pltpu.VMEM((AGG, slots, fine, fine), jnp.float32),
            pltpu.SemaphoreType.DMA,
            pltpu.SemaphoreType.DMA((AGG,)),
        ],
        compiler_params=params,
        cost_estimate=pl.CostEstimate(flops=0, bytes_accessed=8_000_000, transcendentals=0),
        name="split_stiffness",
    )(in_hbm(k_cols), in_hbm(k_vals))

    k_split, pair_other, other_late = lax.optimization_barrier((k_split, pair_other, other))
    pair_near = send(pair_other, toward)
    pair_mine = send(other_late, swap)
    pieces = [mine, pair_mine, *far]

    stiff_shape = (AGG * fine, 256)
    p_shape = (AGG, fine, 256)
    stiff_other = pl.pallas_call(
        stiff_kernel,
        out_shape=jax.ShapeDtypeStruct(stiff_shape, jnp.bfloat16),
        in_specs=[vmem] * 3,
        out_specs=vmem,
        scratch_shapes=[pltpu.VMEM(p_shape, jnp.bfloat16)],
        compiler_params=params,
        cost_estimate=pl.CostEstimate(
            flops=500_000_000, bytes_accessed=1_000_000, transcendentals=0
        ),
        name="stiff_prolong",
    )(other, pair_other, k_split)

    def part_scratch(windows):
        return [pltpu.VMEM((windows, PAIRS, cols_axis, padded, 128), jnp.bfloat16)] * 2

    edge, stiff = pl.pallas_call(
        functools.partial(edge_kernel, cols_axis, padded),
        out_shape=[
            jax.ShapeDtypeStruct((10, padded // 2, 2 * width), jnp.float32),
            jax.ShapeDtypeStruct((2, *stiff_shape), jnp.bfloat16),
        ],
        in_specs=[vmem] * (4 + cols_axis),
        out_specs=[vmem] * 2,
        scratch_shapes=[pltpu.VMEM((2, *p_shape), jnp.bfloat16)] + part_scratch(1),
        compiler_params=params,
        cost_estimate=pl.CostEstimate(
            flops=1_000_000_000, bytes_accessed=2_000_000, transcendentals=0
        ),
        name="edge_terms",
    )(k_split, stiff_other, mine, *far, near, pair_near, pair_mine)
    from_edge = send(edge, away)

    band_shape = jax.ShapeDtypeStruct((5, padded, 2 * width), jnp.float32)
    own, for_pair = pl.pallas_call(
        functools.partial(inner_kernel, cols_axis, padded),
        out_shape=[band_shape] * 2,
        in_specs=[vmem] * (2 + cols_axis),
        out_specs=[vmem] * 2,
        scratch_shapes=part_scratch(2),
        compiler_params=params,
        cost_estimate=pl.CostEstimate(
            flops=500_000_000, bytes_accessed=1_000_000, transcendentals=0
        ),
        name="inner_terms",
    )(stiff_other, stiff, *pieces)
    from_pair = send(for_pair, swap)
    from_pair_edge = send(from_edge[5:], swap)

    coarse = pl.pallas_call(
        functools.partial(sum_kernel, padded),
        out_shape=jax.ShapeDtypeStruct((2, 7, padded, width), jnp.float32),
        in_specs=[vmem] * 4,
        out_specs=vmem,
        compiler_params=params,
        name="sum_terms",
    )(own, from_pair, from_edge, from_pair_edge)
    if padded != share:
        coarse = coarse.reshape(2, 7, padded, cols_axis, padded)[:, :, :share, :, :share]
        coarse = coarse.reshape(2, 7, share, cols_axis * share)
    return jnp.swapaxes(coarse, 2, 3)


def solution(mesh):
    placed = (
        P("row", None, None, None),
        P("row", None),
        P("row", None, None, "col"),
        P("row", None),
    )
    return jax.shard_map(
        functools.partial(body, rows_axis=mesh.shape["row"], cols_axis=mesh.shape["col"]),
        mesh=mesh,
        in_specs=placed,
        out_specs=P("row", None, None, "col"),
        check_vma=False,
    )
```

```python
import functools

import jax
import jax.numpy as jnp
from jax import lax
from jax.experimental import pallas as pl
from jax.experimental.pallas import tpu as pltpu
from jax.sharding import PartitionSpec as P

AGG = 8
PAIRS = AGG // 2


def split_high_low(value):
    high = value.astype(jnp.bfloat16)
    low = (value - high.astype(jnp.float32)).astype(jnp.bfloat16)
    return high, low


def pack_kernel(
    blocks_all, cols_hbm, p_hbm, mine_ref, other_ref, mine_again, other_again,
    cols_ref, p_ref, sems,
):
    cols_copy = pltpu.make_async_copy(cols_hbm, cols_ref, sems.at[0])
    p_copy = pltpu.make_async_copy(p_hbm, p_ref, sems.at[1])
    cols_copy.start()
    p_copy.start()
    half = lax.axis_index("col") % 2
    first_agg = lax.axis_index("row") * 2
    blank = jnp.zeros(p_ref.shape[2:], jnp.float32)
    cols_copy.wait()
    p_copy.wait()
    for part, out_ref, again in ((0, mine_ref, mine_again), (1, other_ref, other_again)):
        group = half if part == 0 else 1 - half
        targets = []
        for window in range(3):
            target = first_agg + group - 1 + window
            targets.append(jnp.where((target >= 0) & (target < blocks_all), target, -2))
        for pair in range(PAIRS):
            rows = []
            for sub in range(2):
                row = group * AGG + 2 * pair + sub
                rows.append([(cols_ref[slot, row], p_ref[row, slot]) for slot in range(3)])
            for window, target in enumerate(targets):
                halves = []
                for slots in rows:
                    value = blank
                    for column, block in slots:
                        value = jnp.where(column == target, block, value)
                    halves.append(value)
                packed = jnp.concatenate(halves, axis=1)
                out_ref[pair, window] = packed
                again[pair, window] = packed


def split_kernel(slots, total_rows, cols_hbm, k_hbm, out_ref, cols_ref, k_ref, cols_sem, sems):
    half = lax.axis_index("col") % 2
    first_row = lax.axis_index("row") * (2 * AGG) + half * AGG
    absent = 3 * AGG

    def k_copy(row):
        return pltpu.make_async_copy(k_hbm.at[half * AGG + row], k_ref.at[row], sems.at[row])

    cols_copy = pltpu.make_async_copy(cols_hbm, cols_ref, cols_sem)
    cols_copy.start()
    for row in range(AGG):
        k_copy(row).start()

    def one_blank(row, carry):
        for column in range(absent):
            out_ref[row, column] = jnp.zeros((64, 128), jnp.bfloat16)
        return carry

    lax.fori_loop(0, AGG, one_blank, 0)
    cols_copy.wait()

    def one_row(row, carry):
        k_copy(row).wait()
        for slot in range(slots):
            column = cols_ref[half * AGG + row, slot]
            present = (column >= 0) & (column < total_rows)
            place = jnp.where(present, column - first_row + AGG, absent)
            place = jnp.clip(place, 0, absent)
            out_ref[row, place] = jnp.concatenate(split_high_low(k_ref[row, slot]), axis=1)
        return carry

    lax.fori_loop(0, AGG, one_row, 0)


def transpose_blocks(sources, p_ref):
    for pair in range(PAIRS):
        block = jnp.concatenate(
            [source[pair, window] for window in range(3) for source in sources],
            axis=0,
        )
        depth = block.shape[0]
        for place, part in enumerate(split_high_low(block.T)):
            for sub in range(2):
                p_ref[2 * pair + sub, :, 128 * place : 128 * place + depth] = part[
                    64 * sub : 64 * sub + 64
                ]


def stiff_product(step, k_ref, p_ref):
    rows = []
    blocks = []
    for row in range(AGG):
        rows.append(k_ref[:, step * AGG + row].reshape(AGG * 64, 128))
        blocks += [p_ref[row], p_ref[row]]
    total = jnp.dot(
        jnp.concatenate(rows, axis=1),
        jnp.concatenate(blocks, axis=0),
        preferred_element_type=jnp.float32,
    )
    return jnp.concatenate(split_high_low(total[:, :128] + total[:, 128:]), axis=1)


def stiff_kernel(other, pair_other, k_ref, out_ref, p_ref):
    half = lax.axis_index("col") % 2
    transpose_blocks((other, pair_other), p_ref)
    out_ref[...] = stiff_product(2 - 2 * half, k_ref, p_ref)


def coarse_terms(stiffs, pieces, windows, share, high_ref, low_ref):
    count = len(pieces)
    width = count * share
    depth = 6 * share
    position = lax.axis_index("col")
    first_half = position % 2 == 0
    for place, window in enumerate(windows):
        for shift in range(count):
            for pair in range(PAIRS):
                high, low = split_high_low(pieces[shift][pair, window])
                high_ref[place, pair, position ^ shift] = high
                low_ref[place, pair, position ^ shift] = low

    def rows_of(part):
        return jnp.concatenate(
            [
                jnp.concatenate(
                    [part[place, pair].reshape(width, 128) for pair in range(PAIRS)], axis=1
                )
                for place in range(len(windows))
            ],
            axis=0,
        )

    high, low = rows_of(high_ref), rows_of(low_ref)
    both = jnp.concatenate([high, low], axis=0)
    rows = len(windows) * width
    totals = []
    for stiff in stiffs:
        total = jnp.dot(both, stiff, preferred_element_type=jnp.float32)
        total = total[:rows] + total[rows:]
        totals.append(total[:, :128] + total[:, 128:])
    mine, other, near = totals
    steps = (jnp.where(first_half, near, other), mine, jnp.where(first_half, other, near))
    terms = [[None] * 5 for _ in windows]
    for step, total in enumerate(steps):
        for place in range(len(windows)):
            turned = total[width * place : width * place + width].T[:depth]
            turned = turned.reshape(3, 2, share, width)
            for slot in range(3):
                before = terms[place][step + slot]
                terms[place][step + slot] = turned[slot] if before is None else before + turned[slot]
    return terms


def edge_kernel(count, share, k_ref, stiff_other, *refs):
    mine = refs[0]
    far = refs[1 : count - 1]
    near, pair_near, pair_mine = refs[count - 1 : count + 2]
    edge_ref, stiff_ref, p_ref, high_ref, low_ref = refs[count + 2 :]
    half = lax.axis_index("col") % 2
    stiffs = []
    for place, step, sources in (
        (0, 1, (mine, pair_mine)),
        (1, 2 * half, (near, pair_near)),
    ):
        transpose_blocks(sources, p_ref.at[place])
        stiffs.append(stiff_product(step, k_ref, p_ref.at[place]))
        stiff_ref[place] = stiffs[place]
    stiffs.insert(1, stiff_other[...])
    pieces = [mine, pair_mine, *far]
    (terms,) = coarse_terms(stiffs, pieces, (2 * half,), share, high_ref, low_ref)
    for slot in range(5):
        for side in range(2):
            term = terms[slot][side]
            folded = jnp.concatenate([term[: share // 2], term[share // 2 :]], axis=1)
            edge_ref[5 * side + slot] = folded


def inner_kernel(count, share, stiff_other, stiff, *refs):
    pieces = refs[:count]
    own_ref, pair_ref, high_ref, low_ref = refs[count:]
    half = lax.axis_index("col") % 2
    width = count * share
    stiffs = [stiff[0], stiff_other[...], stiff[1]]
    windows = (1 - half, 2 - half)
    lower, upper = coarse_terms(stiffs, pieces, windows, share, high_ref, low_ref)
    for side, ref in ((0, own_ref), (1, pair_ref)):
        for slot in range(5):
            ref[slot] = jnp.concatenate([lower[slot][side], upper[slot][side]], axis=1)


def sum_kernel(share, own, from_pair, from_edge, from_pair_edge, out_ref):
    half = lax.axis_index("col") % 2
    width = own.shape[2] // 2

    def unfold(folded):
        return jnp.concatenate([folded[:, :width], folded[:, width:]], axis=0)

    def write(lower, upper, before, after):
        for offset in range(7):
            first = [lower[offset - 1][:, :width]] if 1 <= offset < 6 else []
            first += [upper[offset - 2][:, :width]] if 2 <= offset else []
            first += [unfold(before[offset])] if offset < 5 else []
            out_ref[0, offset] = sum(first[1:], first[0])
            second = [lower[offset][:, width:]] if offset < 5 else []
            second += [upper[offset - 1][:, width:]] if 1 <= offset < 6 else []
            second += [unfold(after[offset - 2])] if 2 <= offset else []
            out_ref[1, offset] = sum(second[1:], second[0])

    @pl.when(half == 0)
    def _():
        write(own, from_pair, from_pair_edge, from_edge)

    @pl.when(half == 1)
    def _():
        write(from_pair, own, from_edge, from_pair_edge)


def body(k_vals, k_cols, p_vals, p_cols, *, rows_axis, cols_axis):
    own_rows, slots, fine, _ = k_vals.shape
    share = p_vals.shape[3]
    padded = -(-share // 16) * 16
    total_rows = own_rows * rows_axis
    blocks_all = total_rows // AGG
    width = cols_axis * padded
    vmem = pl.BlockSpec(memory_space=pltpu.VMEM)
    hbm = pl.BlockSpec(memory_space=pltpu.HBM)
    params = pltpu.CompilerParams(vmem_limit_bytes=24 * 1024 * 1024)

    def in_hbm(value):
        return pltpu.with_memory_space_constraint(value, pltpu.HBM)

    def send(value, target):
        perm = []
        for row in range(rows_axis):
            for col in range(cols_axis):
                to_row, to_col = target(row, col)
                perm.append((row * cols_axis + col, to_row * cols_axis + to_col))
        return lax.ppermute(value, ("row", "col"), perm)

    def toward(row, col):
        return (row + (1 if col % 2 == 0 else -1)) % rows_axis, col

    def away(row, col):
        to_row = row - (1 if col % 2 == 0 else -1)
        return (to_row, col) if 0 <= to_row < rows_axis else swap(row, col)

    def swap(row, col):
        return row, col ^ 1

    p_rows = jnp.swapaxes(p_vals, 2, 3)
    if padded != share:
        p_rows = jnp.pad(p_rows, ((0, 0), (0, 0), (0, padded - share), (0, 0)))
    group_shape = jax.ShapeDtypeStruct((PAIRS, 3, padded, 128), jnp.float32)
    mine, other, mine_again, other_again = pl.pallas_call(
        functools.partial(pack_kernel, blocks_all),
        out_shape=[group_shape] * 4,
        in_specs=[hbm, hbm],
        out_specs=[vmem] * 4,
        scratch_shapes=[
            pltpu.SMEM(p_cols.T.shape, jnp.int32),
            pltpu.VMEM(p_rows.shape, jnp.float32),
            pltpu.SemaphoreType.DMA((2,)),
        ],
        compiler_params=params,
        name="pack_window",
    )(in_hbm(p_cols.T), in_hbm(p_rows))

    pair_other = send(mine, swap)
    far = []
    for shift in range(2, cols_axis):
        far.append(
            send(mine_again if shift % 2 == 0 else other_again, lambda row, col: (row, col ^ shift))
        )
    near = send(other, toward)
    k_split = pl.pallas_call(
        functools.partial(split_kernel, slots, total_rows),
        out_shape=jax.ShapeDtypeStruct((AGG, 3 * AGG + 1, fine, 128), jnp.bfloat16),
        in_specs=[hbm, hbm],
        out_specs=vmem,
        scratch_shapes=[
            pltpu.SMEM(k_cols.shape, jnp.int32),
            pltpu.VMEM((AGG, slots, fine, fine), jnp.float32),
            pltpu.SemaphoreType.DMA,
            pltpu.SemaphoreType.DMA((AGG,)),
        ],
        compiler_params=params,
        cost_estimate=pl.CostEstimate(flops=0, bytes_accessed=8_000_000, transcendentals=0),
        name="split_stiffness",
    )(in_hbm(k_cols), in_hbm(k_vals))

    pair_near = send(pair_other, toward)
    pair_mine = send(other, swap)
    pieces = [mine, pair_mine, *far]

    stiff_shape = (AGG * fine, 256)
    p_shape = (AGG, fine, 256)
    stiff_other = pl.pallas_call(
        stiff_kernel,
        out_shape=jax.ShapeDtypeStruct(stiff_shape, jnp.bfloat16),
        in_specs=[vmem] * 3,
        out_specs=vmem,
        scratch_shapes=[pltpu.VMEM(p_shape, jnp.bfloat16)],
        compiler_params=params,
        cost_estimate=pl.CostEstimate(
            flops=500_000_000, bytes_accessed=1_000_000, transcendentals=0
        ),
        name="stiff_prolong",
    )(other, pair_other, k_split)

    def part_scratch(windows):
        return [pltpu.VMEM((windows, PAIRS, cols_axis, padded, 128), jnp.bfloat16)] * 2

    edge, stiff = pl.pallas_call(
        functools.partial(edge_kernel, cols_axis, padded),
        out_shape=[
            jax.ShapeDtypeStruct((10, padded // 2, 2 * width), jnp.float32),
            jax.ShapeDtypeStruct((2, *stiff_shape), jnp.bfloat16),
        ],
        in_specs=[vmem] * (4 + cols_axis),
        out_specs=[vmem] * 2,
        scratch_shapes=[pltpu.VMEM((2, *p_shape), jnp.bfloat16)] + part_scratch(1),
        compiler_params=params,
        cost_estimate=pl.CostEstimate(
            flops=1_000_000_000, bytes_accessed=2_000_000, transcendentals=0
        ),
        name="edge_terms",
    )(k_split, stiff_other, mine, *far, near, pair_near, pair_mine)
    from_edge = send(edge, away)

    band_shape = jax.ShapeDtypeStruct((5, padded, 2 * width), jnp.float32)
    own, for_pair = pl.pallas_call(
        functools.partial(inner_kernel, cols_axis, padded),
        out_shape=[band_shape] * 2,
        in_specs=[vmem] * (2 + cols_axis),
        out_specs=[vmem] * 2,
        scratch_shapes=part_scratch(2),
        compiler_params=params,
        cost_estimate=pl.CostEstimate(
            flops=500_000_000, bytes_accessed=1_000_000, transcendentals=0
        ),
        name="inner_terms",
    )(stiff_other, stiff, *pieces)
    from_pair = send(for_pair, swap)
    from_pair_edge = send(from_edge[5:], swap)

    coarse = pl.pallas_call(
        functools.partial(sum_kernel, padded),
        out_shape=jax.ShapeDtypeStruct((2, 7, padded, width), jnp.float32),
        in_specs=[vmem] * 4,
        out_specs=vmem,
        compiler_params=params,
        name="sum_terms",
    )(own, from_pair, from_edge, from_pair_edge)
    if padded != share:
        coarse = coarse.reshape(2, 7, padded, cols_axis, padded)[:, :, :share, :, :share]
        coarse = coarse.reshape(2, 7, share, cols_axis * share)
    return jnp.swapaxes(coarse, 2, 3)


def solution(mesh):
    placed = (
        P("row", None, None, None),
        P("row", None),
        P("row", None, None, "col"),
        P("row", None),
    )
    return jax.shard_map(
        functools.partial(body, rows_axis=mesh.shape["row"], cols_axis=mesh.shape["col"]),
        mesh=mesh,
        in_specs=placed,
        out_specs=P("row", None, None, "col"),
        check_vma=False,
    )
```
